256 devices in a mesh: band: 64 (over z, x, core), tm: 4 (over y).
Axes of the slice: x: 4, y: 4, z: 8, core: 2. Of those that a mesh axis runs over, the one named last changes fastest.
Arguments:
- spectra: float32 [64, 64, 16384], P(None, 'band', 'tm'), may hold values from -6 to 6
- newest: float32 [64, 64, 4, 1024], P(None, 'band', 'tm')
- ingest_owner: int32 [64], P('band'), may hold values from 0 to 3
- low_trial: int32 [4, 4096], P(None, 'band'), may hold values from 0 to 7, as said below
- high_trial: int32 [4, 4096], P(None, 'band'), may hold values from 0 to 7, as said below
- delay_table: int32 [4, 4096], P(None, 'band'), may hold values from 0 to 64, as said below
Outputs:
- dedispersed: float32 [256, 16, 16384], P('band', None, 'tm')
The draws below stay inside these ranges and needn't reach their ends.
Inputs may be any that keep to these rules, and one draw needn't show every extreme that they name: `low_trial`: at level l (row l-1) entry r belongs to trial r % 2^l and names a trial below 2^(l-1); the highest trial of each subband names trial 2^(l-1) - 1. `high_trial`: as low_trial, for the upper half-subband. `delay_table`: at level l the delays are at most 8 * 2^(l-1), reached by the highest trial of each subband.
All inputs are finite; a program needn't handle non-finite values.
Results may differ from the reference program's by a relative error of at most 0.0003.
Values sent between devices are 32-bit elements; how exact they have to be, the bound alone decides.
A program may use at most 64 MiB of HBM per device.

```python
import math
import jax
import jax.numpy as jnp
from jax import lax

CH_DEV = 64
BLOCK = 1024
LEVELS = 4
SHIFT = 8
CHANNELS = 4096
TIME = 16384
TRIALS = 16
SUBBANDS = 256
N_BAND = 64
N_TM = 4


def level_layout():
    layer_ids = jnp.arange(LEVELS, dtype=jnp.int32)[:, None]
    half_span = jnp.left_shift(jnp.ones_like(layer_ids), layer_ids)
    column_ids = jnp.arange(CHANNELS, dtype=jnp.int32)[None, :]
    trial_ids = column_ids % (2 * half_span)
    return (half_span, trial_ids)


def trial_table(key_table):
    half_span, trial_ids = level_layout()
    raw_values = jax.random.randint(key_table, (LEVELS, CHANNELS), 0, 65536, dtype=jnp.int32) % half_span
    return jnp.where(trial_ids == 2 * half_span - 1, half_span - 1, raw_values).astype(jnp.int32)


def draw_low_trial(key, part):
    key = jax.random.fold_in(key, 3)
    return trial_table(key)


def draw_high_trial(key, part):
    key = jax.random.fold_in(key, 5)
    return trial_table(key)


def draw_delay_table(key, part):
    key = jax.random.fold_in(key, 7)
    half_span, trial_ids = level_layout()
    reach_max = SHIFT * half_span
    raw_values = jax.random.randint(key, (LEVELS, CHANNELS), 0, 1 << 20, dtype=jnp.int32) % (reach_max + 1)
    return jnp.where(trial_ids == 2 * half_span - 1, reach_max, raw_values).astype(jnp.int32)


def draw_newest(key, part):
    key = jax.random.fold_in(key, 11)
    key_noise, key_offset, key_scale = jax.random.split(key, 3)
    full_shape = (CH_DEV, N_BAND, N_TM, BLOCK)
    row_shape = (CH_DEV, N_BAND, N_TM, 1)
    noise = jax.random.normal(key_noise, full_shape, jnp.float32)
    offset = jax.random.uniform(key_offset, row_shape, jnp.float32, -2.0, 2.0)
    scale = jnp.exp(jax.random.uniform(key_scale, row_shape, jnp.float32, math.log(0.25), math.log(4.0)))
    return (offset + scale * noise).astype(jnp.float32)


def set_ends(values, stream_key, least, high):
    shape = values.shape
    place = [jax.random.randint(jax.random.fold_in(stream_key, axis), (), 0, shape[axis]) for axis in range(len(shape))]
    values = values.at[tuple(place)].set(least)
    longest = shape.index(max(shape))
    place[longest] = (place[longest] + 1) % shape[longest]
    return values.at[tuple(place)].set(high)


def steps_of(own_key, extent, cuts, low, top_value):
    loudness = 1.0
    for position, blocks in cuts:
        draws = jax.random.uniform(jax.random.fold_in(jax.random.fold_in(own_key, 6), position), (blocks,), jnp.float32, low / len(cuts), top_value / len(cuts))
        loudness = loudness * jnp.repeat(jnp.exp(draws), extent[position] // blocks).reshape((-1,) + (1,) * (len(extent) - 1 - position))
    return loudness


def gaussian(stream_key, shape, spread, reach, pieces=(), kind=jnp.bfloat16):
    values = spread * jax.random.normal(stream_key, shape, jnp.float32)
    if pieces:
        values = values * steps_of(stream_key, shape, pieces, -0.22, 0.18)
    return jnp.clip(values, -reach, reach).astype(kind)


def setup_inputs(seed: int = 0) -> dict:
    splits = jax.random.split(jax.random.key(seed), 7)
    spectra = gaussian(splits[0], (CH_DEV, N_BAND, TIME), 1.0, 6.0, ((1, 64), (2, 4)), jnp.float32)
    newest = draw_newest(jax.random.fold_in(splits[6], 71), 0)
    ingest_owner = set_ends(jax.random.randint(splits[2], (N_BAND,), 0, N_TM), jax.random.fold_in(splits[2], 1), 0, N_TM - 1).astype(jnp.int32)
    low_trial = draw_low_trial(jax.random.fold_in(splits[6], 71), 0)
    high_trial = draw_high_trial(jax.random.fold_in(splits[6], 71), 0)
    delay_table = draw_delay_table(jax.random.fold_in(splits[6], 71), 0)
    return {"spectra": spectra, "newest": newest, "ingest_owner": ingest_owner, "low_trial": low_trial, "high_trial": high_trial, "delay_table": delay_table}


def channel_stats(ingest):
    block_mean = lax.optimization_barrier(jnp.mean(ingest, axis=-1))
    centred = ingest - block_mean[:, None]
    inv_scale = 1.0 / jnp.sqrt(lax.optimization_barrier(jnp.mean(centred * centred, axis=-1)) + 1e-06)
    return (block_mean, inv_scale)

def delayed_rows(source, shifts, length):
    reach_max = source.shape[1] - length
    shifted = source
    for bit_pos in range(reach_max.bit_length()):
        step_size = 1 << bit_pos
        moved = jnp.concatenate([jnp.zeros((source.shape[0], step_size), source.dtype), shifted[:, :-step_size]], axis=1)
        flags = jnp.right_shift(shifts.astype(jnp.int32), bit_pos) % 2 == 1
        shifted = jnp.where(flags[:, None], moved, shifted)
    return shifted[:, reach_max:]

def merge_levels(current, low_table, high_table, shift_rows, shift_unit, levels):
    row_ids = jnp.arange(current.shape[0], dtype=jnp.int32)
    length = current.shape[1]
    for layer_idx in range(levels):
        half_span = 2 ** layer_idx
        span_width = 2 * half_span
        base_rows = row_ids // span_width * span_width
        low_rows = base_rows + low_table[layer_idx]
        high_rows = base_rows + half_span + high_table[layer_idx]
        reach_max = shift_unit * half_span
        padded = jnp.pad(current[high_rows], ((0, 0), (reach_max, 0)))
        current = current[low_rows] + delayed_rows(padded, shift_rows[layer_idx], length)
    return current

def reference(spectra, newest, ingest_owner, low_trial, high_trial, delay_table):
    owner_index = jnp.broadcast_to(ingest_owner.astype(jnp.int32)[None, :, None, None], (CH_DEV, N_BAND, 1, BLOCK))
    ingest = jnp.take_along_axis(newest, owner_index, axis=2)[:, :, 0, :].reshape(CHANNELS, BLOCK)
    block_mean, inv_scale = channel_stats(ingest)
    normed = (spectra.reshape(CHANNELS, TIME) - block_mean[:, None]) * inv_scale[:, None]
    groups = normed.reshape(SUBBANDS, TRIALS, TIME)

    def regroup_table(table):
        return table.reshape(LEVELS, SUBBANDS, TRIALS).transpose(1, 0, 2)

    def one_group(packed):
        return merge_levels(packed[0], packed[1], packed[2], packed[3], SHIFT, LEVELS)
    return lax.map(one_group, (groups, regroup_table(low_trial), regroup_table(high_trial), regroup_table(delay_table)))
```

```python
import functools

import jax
import jax.numpy as jnp
from jax import lax
from jax.experimental import pallas as pl
from jax.experimental.pallas import tpu as pltpu
from jax.sharding import PartitionSpec as P

LEVELS = 4
NB, NT = 64, 4
NZ, NX, NC = 8, 4, 2
TILES = 32
CHUNK = 8
FIRST = 8
STAT = FIRST + TILES
ROWS = STAT + 8
ORDER = (0, 3, 1, 2)
MESH = pl.DeviceIdType.MESH


def partner(me, step):
    j, r = step % NZ, step // NZ
    dz = (1 - 2 * (j % 2)) * ((j + 1) // 2)
    z, q = me // (NX * NC), me % (NX * NC)
    x, c = q // NC, q % NC
    return ((z + dz + NZ) % NZ) * (NX * NC) + ((x + r // NC) % NX) * NC + (c + r % NC) % NC


def kernel(
    x_ref, newest_ref, owner_ref, low_ref, high_ref, delay_ref, out_ref,
    buf, tail, fresh, gathered, s1, s2, s3, owner, low, high, delay,
    local_sem, table_sem, send_sem, recv_sem, stat_send, stat_recv, halo_send, halo_recv,
):
    me, t = lax.axis_index("band"), lax.axis_index("tm")
    loads = [
        pltpu.make_async_copy(newest_ref, fresh, local_sem.at[0]),
        pltpu.make_async_copy(x_ref.at[:, pl.ds(TILES - CHUNK, CHUNK)], tail.at[:, pl.ds(0, CHUNK)], local_sem.at[1]),
    ]
    tables = [
        pltpu.make_async_copy(src, dst, table_sem.at[i])
        for i, (src, dst) in enumerate(((owner_ref, owner), (low_ref, low), (high_ref, high), (delay_ref, delay)))
    ]
    for copy in loads + tables:
        copy.start()

    barrier = pltpu.get_barrier_semaphore()

    @pl.loop(1, NB)
    def _(i):
        pl.semaphore_signal(barrier, inc=1, device_id={"band": (me + i) % NB}, device_id_type=MESH)

    for i in range(1, NT):
        pl.semaphore_signal(barrier, inc=1, device_id={"tm": (t + i) % NT}, device_id_type=MESH)
    pl.semaphore_wait(barrier, NB - 1 + NT - 1)

    def spans(c):
        if c == TILES // CHUNK - 1:
            return tail, pl.ds(0, CHUNK + 2), pl.ds(FIRST + c * CHUNK, CHUNK + 2)
        return x_ref, pl.ds(c * CHUNK, CHUNK), pl.ds(FIRST + c * CHUNK, CHUNK)

    def send(c):
        src, here, there = spans(c)

        @pl.loop(1, NB)
        def _(i):
            peer = partner(me, i)
            pltpu.make_async_remote_copy(
                src_ref=src.at[peer, here], dst_ref=buf.at[me, there], send_sem=send_sem.at[c],
                recv_sem=recv_sem.at[c], device_id={"band": peer}, device_id_type=MESH,
            ).start()

        pltpu.make_async_copy(src.at[me, here], buf.at[me, there], recv_sem.at[c]).start()

    def arrive(c):
        src, here, there = spans(c)
        pltpu.make_async_copy(src.at[:, here], buf.at[:, there], recv_sem.at[c]).wait()

    send(ORDER[0])

    loads[0].wait()
    block = fresh[...]
    total = jnp.sum(jnp.sum(block, axis=1), axis=-1, keepdims=True)
    mean = total * (1.0 / (8 * 128))
    centred = block - mean[:, :, None]
    power = jnp.sum(jnp.sum(centred * centred, axis=1), axis=-1, keepdims=True) * (1.0 / (8 * 128))
    inv = 1.0 / jnp.sqrt(power + 1e-6)
    gathered[t, 0] = jnp.broadcast_to(mean, (NB, 128))
    gathered[t, 1] = jnp.broadcast_to(inv, (NB, 128))
    stat_copies = []
    for i in range(1, NT):
        stat_copies.append(pltpu.make_async_remote_copy(
            src_ref=gathered.at[t], dst_ref=gathered.at[t], send_sem=stat_send.at[i - 1], recv_sem=stat_recv.at[i - 1],
            device_id={"tm": (t + i) % NT}, device_id_type=MESH,
        ))
        stat_copies[-1].start()
    for copy in tables:
        copy.wait()
    for i in range(1, NT):
        pltpu.make_async_copy(gathered.at[0], gathered.at[0], stat_recv.at[i - 1]).wait()
    chosen = gathered[0]
    for i in range(1, NT):
        chosen = jnp.where(owner[0] == i, gathered[i], chosen)
    loads[1].wait()
    tail[:, CHUNK, :] = chosen[0]
    tail[:, CHUNK + 1, :] = chosen[1]

    for c in ORDER[1:]:
        send(c)

    lane = lax.broadcasted_iota(jnp.int32, (CHUNK, 128), 1)
    sub = lax.broadcasted_iota(jnp.int32, (CHUNK, 128), 0)

    def delayed(high_now, high_before, d):
        return pltpu.roll(jnp.where(lane < 128 - d, high_now, high_before), d, 1)

    def first_level(c):
        now = pl.ds(FIRST + c * CHUNK, CHUNK)
        before = pl.ds(FIRST + c * CHUNK - 1, CHUNK)

        @pl.loop(0, NB // 16)
        def _(g):
            for p in range(8):
                even = g * 16 + 2 * p
                odd = even + 1
                mean_e, inv_e = buf[even, pl.ds(STAT, 1)], buf[even, pl.ds(STAT + 1, 1)]
                mean_o, inv_o = buf[odd, pl.ds(STAT, 1)], buf[odd, pl.ds(STAT + 1, 1)]
                base = (buf[even, now] - mean_e) * inv_e
                n_now = (buf[odd, now] - mean_o) * inv_o
                n_before = (buf[odd, before] - mean_o) * inv_o
                if c == 0:
                    n_before = jnp.where((sub > 0) | (t > 0), n_before, 0.0)
                for k in range(2):
                    s1[even + k, now] = base + delayed(n_now, n_before, delay[0, even + k])

    def later_level(level, src, c, store):
        now = pl.ds(FIRST + c * CHUNK, CHUNK)
        before = pl.ds(FIRST + c * CHUNK - 1, CHUNK)
        half = 2**level

        @pl.loop(0, NB // 16)
        def _(g):
            for p in range(16):
                r = g * 16 + p
                base = g * 16 + p // (2 * half) * (2 * half)
                lo = base + low[level, r]
                hi = base + half + high[level, r]
                store(r, src[lo, now] + delayed(src[hi, now], src[hi, before], delay[level, r]))

    def halo_levels():
        spot = pl.ds(FIRST - 1, 1)

        @pl.loop(0, NB // 16)
        def _(g):
            for p in range(8):
                even = g * 16 + 2 * p
                odd = even + 1
                base = (buf[even, spot] - buf[even, pl.ds(STAT, 1)]) * buf[even, pl.ds(STAT + 1, 1)]
                over = (buf[odd, spot] - buf[odd, pl.ds(STAT, 1)]) * buf[odd, pl.ds(STAT + 1, 1)]
                for k in range(2):
                    s1[even + k, spot] = jnp.where(t > 0, base + pltpu.roll(over, delay[0, even + k], 1), 0.0)

        for level, src, dst in ((1, s1, s2), (2, s2, s3)):
            half = 2**level

            @pl.loop(0, NB // 16)
            def _(g):
                for p in range(16):
                    r = g * 16 + p
                    base = g * 16 + p // (2 * half) * (2 * half)
                    lo = base + low[level, r]
                    hi = base + half + high[level, r]
                    dst[r, spot] = src[lo, spot] + pltpu.roll(src[hi, spot], delay[level, r], 1)

    def levels(c):
        now = pl.ds(FIRST + c * CHUNK, CHUNK)

        def keep(dst):
            def store(r, value):
                dst[r, now] = value
            return store

        def final(r, value):
            out_ref[r, pl.ds(c * CHUNK, CHUNK)] = value

        first_level(c)
        later_level(1, s1, c, keep(s2))
        later_level(2, s2, c, keep(s3))
        later_level(3, s3, c, final)

    arrive(0)
    arrive(3)
    halo = pltpu.make_async_remote_copy(
        src_ref=buf.at[:, pl.ds(STAT - 1, 1)], dst_ref=buf.at[:, pl.ds(FIRST - 1, 1)], send_sem=halo_send,
        recv_sem=halo_recv, device_id={"tm": (t + 1) % NT}, device_id_type=MESH,
    )
    halo.start()
    halo.wait_recv()
    halo_levels()
    levels(0)
    arrive(1)
    levels(1)
    arrive(2)
    levels(2)
    levels(3)

    halo.wait_send()
    for copy in stat_copies:
        copy.wait_send()
    for c in ORDER:
        src, here, there = spans(c)
        pltpu.make_async_copy(src.at[pl.ds(0, NB - 1), here], buf.at[pl.ds(0, NB - 1), there], send_sem.at[c]).wait()


def shards(spectra, newest, ingest_owner, low_trial, high_trial, delay_table):
    state = pltpu.VMEM((NB, ROWS, 128), jnp.float32)
    out = pl.pallas_call(
        kernel,
        out_shape=jax.ShapeDtypeStruct((NB, TILES, 128), jnp.float32),
        in_specs=[pl.BlockSpec(memory_space=pl.ANY)] * 6,
        out_specs=pl.BlockSpec(memory_space=pltpu.VMEM),
        scratch_shapes=[
            state,
            pltpu.VMEM((NB, 2 * CHUNK, 128), jnp.float32),
            pltpu.VMEM((NB, 8, 128), jnp.float32),
            pltpu.VMEM((NT, 2, NB, 128), jnp.float32),
            state, state, state,
            pltpu.SMEM((1,), jnp.int32),
            pltpu.SMEM((LEVELS, NB), jnp.int32),
            pltpu.SMEM((LEVELS, NB), jnp.int32),
            pltpu.SMEM((LEVELS, NB), jnp.int32),
            pltpu.SemaphoreType.DMA((2,)),
            pltpu.SemaphoreType.DMA((4,)),
            pltpu.SemaphoreType.DMA((TILES // CHUNK,)),
            pltpu.SemaphoreType.DMA((TILES // CHUNK,)),
            pltpu.SemaphoreType.DMA((NT - 1,)),
            pltpu.SemaphoreType.DMA((NT - 1,)),
            pltpu.SemaphoreType.DMA,
            pltpu.SemaphoreType.DMA,
        ],
        compiler_params=pltpu.CompilerParams(collective_id=1, has_side_effects=True, vmem_limit_bytes=24 << 20),
    )(spectra.reshape(NB, TILES, 128), newest.reshape(NB, 8, 128), ingest_owner, low_trial, high_trial, delay_table)
    return out.reshape(NB // 16, 16, TILES * 128)


def solution(mesh):
    return jax.shard_map(
        shards,
        mesh=mesh,
        in_specs=(
            P(None, "band", "tm"),
            P(None, "band", "tm", None),
            P("band"),
            P(None, "band"),
            P(None, "band"),
            P(None, "band"),
        ),
        out_specs=P("band", None, "tm"),
        check_vma=False,
    )
```

```python
import functools

import jax
import jax.numpy as jnp
from jax import lax
from jax.experimental import pallas as pl
from jax.experimental.pallas import tpu as pltpu
from jax.sharding import PartitionSpec as P

LEVELS = 4
NB, NT = 64, 4
NZ, NQ = 8, 8
TILES = 32
CHUNK = 8
FIRST = 8
STAT = FIRST + TILES
ROWS = STAT + 8
SPANS = ((0, 8), (8, 8), (16, 8), (24, 7))
HEAD = len(SPANS)
PLAN = [(k, c) for c in range(HEAD) for k in range(NZ)]
UNROLL = 4
MESH = pl.DeviceIdType.MESH


def kernel(
    x_ref, newest_ref, owner_ref, low_ref, high_ref, delay_ref, out_ref,
    buf, tail, fresh, gathered, means, invs, s1, s2, s3, owner, low, high, delay,
    local_sem, table_sem, send_sem, recv_sem, stat_send, stat_recv, halo_send, halo_recv,
):
    me, t = lax.axis_index("band"), lax.axis_index("tm")
    loads = [
        pltpu.make_async_copy(newest_ref, fresh, local_sem.at[0]),
        pltpu.make_async_copy(x_ref.at[:, pl.ds(TILES - 1, 1)], tail.at[:, pl.ds(0, 1)], local_sem.at[1]),
    ]
    tables = [
        pltpu.make_async_copy(src, dst, table_sem.at[i])
        for i, (src, dst) in enumerate(((owner_ref, owner), (low_ref, low), (high_ref, high), (delay_ref, delay)))
    ]
    for copy in loads + tables:
        copy.start()

    barrier = pltpu.get_barrier_semaphore()
    for i in range(1, NB):
        peer = me + i
        pl.semaphore_signal(
            barrier, inc=1, device_id={"band": jnp.where(peer < NB, peer, peer - NB)}, device_id_type=MESH
        )
    for i in range(1, NT):
        pl.semaphore_signal(barrier, inc=1, device_id={"tm": (t + i) % NT}, device_id_type=MESH)

    def spans(c):
        if c == HEAD:
            return tail, pl.ds(0, 2), pl.ds(STAT - 1, 2)
        start, size = SPANS[c]
        return x_ref, pl.ds(start, size), pl.ds(FIRST + start, size)

    z = me // NQ
    q = me - z * NQ
    turned = [jnp.where(q + r < NQ, q + r, q + r - NQ) for r in range(NQ)]

    def send(k, c):
        src, here, there = spans(c)

        def one(peer):
            pltpu.make_async_remote_copy(
                src_ref=src.at[peer, here], dst_ref=buf.at[me, there], send_sem=send_sem.at[c],
                recv_sem=recv_sem.at[c], device_id={"band": peer}, device_id_type=MESH,
            ).start()

        pl.when(k != z)(lambda: one(k * NQ + q))
        for r in range(1, NQ):
            one(k * NQ + turned[r])

    def keep_own(c):
        src, here, there = spans(c)
        pltpu.make_async_copy(src.at[me, here], buf.at[me, there], recv_sem.at[c]).start()

    def arrive(c):
        src, here, there = spans(c)
        pltpu.make_async_copy(src.at[:, here], buf.at[:, there], recv_sem.at[c]).wait()

    for c in range(HEAD):
        keep_own(c)

    loads[0].wait()
    block = fresh[...]
    total = jnp.sum(jnp.sum(block, axis=1), axis=-1, keepdims=True)
    mean = total * (1.0 / (8 * 128))
    centred = block - mean[:, :, None]
    power = jnp.sum(jnp.sum(centred * centred, axis=1), axis=-1, keepdims=True) * (1.0 / (8 * 128))
    inv = 1.0 / jnp.sqrt(power + 1e-6)
    row = lax.broadcasted_iota(jnp.int32, (NB, 128), 0)
    column = lax.broadcasted_iota(jnp.int32, (NB, 128), 1)
    both = jnp.where(column == row, mean, 0.0) + jnp.where(column == row + NB, inv, 0.0)
    for copy in tables:
        copy.wait()
    mine = jnp.where(owner[0] == t, jnp.sum(both, axis=0, keepdims=True), 0.0)
    loads[1].wait()
    tail[:, 1, :] = jnp.broadcast_to(mine, (NB, 128))
    pl.semaphore_wait(barrier, NB - 1 + NT - 1)

    for k in range(NZ):
        send(k, HEAD)
    keep_own(HEAD)
    for k, c in PLAN:
        send(k, c)

    lane = lax.broadcasted_iota(jnp.int32, (CHUNK, 128), 1)
    sub = lax.broadcasted_iota(jnp.int32, (CHUNK, 128), 0)

    def delayed(high_now, high_before, d):
        return pltpu.roll(jnp.where(lane < 128 - d, high_now, high_before), d, 1)

    def first_level(c):
        now = pl.ds(FIRST + c * CHUNK, CHUNK)
        before = pl.ds(FIRST + c * CHUNK - 1, CHUNK)

        @pl.loop(0, NB // 16 // UNROLL)
        def _(g):
            for p in range(8 * UNROLL):
                even = g * 16 * UNROLL + 2 * p
                odd = even + 1
                mean_e, inv_e = means[pl.ds(even, 1)], invs[pl.ds(even, 1)]
                mean_o, inv_o = means[pl.ds(odd, 1)], invs[pl.ds(odd, 1)]
                base = (buf[even, now] - mean_e) * inv_e
                n_now = (buf[odd, now] - mean_o) * inv_o
                n_before = (buf[odd, before] - mean_o) * inv_o
                if c == 0:
                    n_before = jnp.where((sub > 0) | (t > 0), n_before, 0.0)
                for k in range(2):
                    s1[even + k, now] = base + delayed(n_now, n_before, delay[0, even + k])

    def later_level(level, src, c, store):
        now = pl.ds(FIRST + c * CHUNK, CHUNK)
        before = pl.ds(FIRST + c * CHUNK - 1, CHUNK)
        half = 2**level

        @pl.loop(0, NB // 16 // UNROLL)
        def _(g):
            for p in range(16 * UNROLL):
                r = g * 16 * UNROLL + p
                base = g * 16 * UNROLL + p // (2 * half) * (2 * half)
                lo = base + low[level, r]
                hi = base + half + high[level, r]
                store(r, src[lo, now] + delayed(src[hi, now], src[hi, before], delay[level, r]))

    def halo_levels():
        spot = pl.ds(FIRST - 1, 1)

        @pl.loop(0, NB // 16 // UNROLL)
        def _(g):
            for p in range(8 * UNROLL):
                even = g * 16 * UNROLL + 2 * p
                odd = even + 1
                base = (buf[even, spot] - means[pl.ds(even, 1)]) * invs[pl.ds(even, 1)]
                over = (buf[odd, spot] - means[pl.ds(odd, 1)]) * invs[pl.ds(odd, 1)]
                for k in range(2):
                    s1[even + k, spot] = jnp.where(t > 0, base + pltpu.roll(over, delay[0, even + k], 1), 0.0)

        for level, src, dst in ((1, s1, s2), (2, s2, s3)):
            half = 2**level

            @pl.loop(0, NB // 16 // UNROLL)
            def _(g):
                for p in range(16 * UNROLL):
                    r = g * 16 * UNROLL + p
                    base = g * 16 * UNROLL + p // (2 * half) * (2 * half)
                    lo = base + low[level, r]
                    hi = base + half + high[level, r]
                    dst[r, spot] = src[lo, spot] + pltpu.roll(src[hi, spot], delay[level, r], 1)

    def levels(c):
        now = pl.ds(FIRST + c * CHUNK, CHUNK)

        def keep(dst):
            def store(r, value):
                dst[r, now] = value
            return store

        def final(r, value):
            out_ref[r, pl.ds(c * CHUNK, CHUNK)] = value

        first_level(c)
        later_level(1, s1, c, keep(s2))
        later_level(2, s2, c, keep(s3))
        later_level(3, s3, c, final)

    arrive(HEAD)
    halo = pltpu.make_async_remote_copy(
        src_ref=buf.at[:, pl.ds(STAT - 1, 1)], dst_ref=buf.at[:, pl.ds(FIRST - 1, 1)], send_sem=halo_send,
        recv_sem=halo_recv, device_id={"tm": (t + 1) % NT}, device_id_type=MESH,
    )
    halo.start()
    stat = buf[:, STAT, :]
    mean = jnp.sum(jnp.where(column == me, stat, 0.0), axis=1, keepdims=True)
    inv = jnp.sum(jnp.where(column == me + NB, stat, 0.0), axis=1, keepdims=True)
    both = jnp.where(column == row, mean, 0.0) + jnp.where(column == row + NB, inv, 0.0)
    gathered[pl.ds(t, 1)] = jnp.sum(both, axis=0, keepdims=True)[None]
    stat_copies = []
    for i in range(1, NT):
        stat_copies.append(pltpu.make_async_remote_copy(
            src_ref=gathered.at[t], dst_ref=gathered.at[t], send_sem=stat_send.at[i - 1], recv_sem=stat_recv.at[i - 1],
            device_id={"tm": (t + i) % NT}, device_id_type=MESH,
        ))
        stat_copies[-1].start()
    for copy in stat_copies:
        copy.wait_recv()
    stat = gathered[0]
    for i in range(1, NT):
        stat = stat + gathered[i]
    mean = jnp.sum(jnp.where(column == row, stat, 0.0), axis=1, keepdims=True)
    inv = jnp.sum(jnp.where(column == row + NB, stat, 0.0), axis=1, keepdims=True)
    means[...] = jnp.broadcast_to(mean, (NB, 128))
    invs[...] = jnp.broadcast_to(inv, (NB, 128))
    halo.wait_recv()
    halo_levels()
    for c, (start, size) in enumerate(SPANS):
        arrive(c)
        for block in range(start // CHUNK, (start + size + 1) // CHUNK):
            levels(block)

    halo.wait_send()
    for copy in stat_copies:
        copy.wait_send()
    for c in range(HEAD + 1):
        src, here, there = spans(c)
        pltpu.make_async_copy(src.at[pl.ds(0, NB - 1), here], buf.at[pl.ds(0, NB - 1), there], send_sem.at[c]).wait()


def shards(spectra, newest, ingest_owner, low_trial, high_trial, delay_table):
    operands = [spectra.reshape(NB, TILES, 128), newest.reshape(NB, 8, 128), ingest_owner, low_trial, high_trial, delay_table]
    operands = [a if a.size == 1 else pltpu.with_memory_space_constraint(a, pltpu.HBM) for a in operands]
    state = pltpu.VMEM((NB, ROWS, 128), jnp.float32)
    out = pl.pallas_call(
        kernel,
        out_shape=jax.ShapeDtypeStruct((NB, TILES, 128), jnp.float32),
        in_specs=[pl.BlockSpec(memory_space=pl.ANY)] * 6,
        out_specs=pl.BlockSpec(memory_space=pltpu.VMEM),
        scratch_shapes=[
            state,
            pltpu.VMEM((NB, 8, 128), jnp.float32),
            pltpu.VMEM((NB, 8, 128), jnp.float32),
            pltpu.VMEM((NT, 1, 128), jnp.float32),
            pltpu.VMEM((NB, 128), jnp.float32),
            pltpu.VMEM((NB, 128), jnp.float32),
            state, state, state,
            pltpu.SMEM((1,), jnp.int32),
            pltpu.SMEM((LEVELS, NB), jnp.int32),
            pltpu.SMEM((LEVELS, NB), jnp.int32),
            pltpu.SMEM((LEVELS, NB), jnp.int32),
            pltpu.SemaphoreType.DMA((2,)),
            pltpu.SemaphoreType.DMA((4,)),
            pltpu.SemaphoreType.DMA((HEAD + 1,)),
            pltpu.SemaphoreType.DMA((HEAD + 1,)),
            pltpu.SemaphoreType.DMA((NT - 1,)),
            pltpu.SemaphoreType.DMA((NT - 1,)),
            pltpu.SemaphoreType.DMA,
            pltpu.SemaphoreType.DMA,
        ],
        compiler_params=pltpu.CompilerParams(collective_id=1, has_side_effects=True, vmem_limit_bytes=24 << 20),
    )(*operands)
    return out.reshape(NB // 16, 16, TILES * 128)


def solution(mesh):
    return jax.shard_map(
        shards,
        mesh=mesh,
        in_specs=(
            P(None, "band", "tm"),
            P(None, "band", "tm", None),
            P("band"),
            P(None, "band"),
            P(None, "band"),
            P(None, "band"),
        ),
        out_specs=P("band", None, "tm"),
        check_vma=False,
    )
```

```python
import functools

import jax
import jax.numpy as jnp
from jax import lax
from jax.experimental import pallas as pl
from jax.experimental.pallas import tpu as pltpu
from jax.sharding import PartitionSpec as P

LEVELS = 4
NB, NT = 64, 4
NZ, NQ = 8, 8
TILES = 32
CHUNK = 8
FIRST = 8
ROWS = FIRST + TILES
SPANS = ((0, 16), (16, 15))
HEAD = len(SPANS)
PLAN = [(k, c) for c in range(HEAD) for k in range(NZ)]
MESH = pl.DeviceIdType.MESH


def kernel(
    x_ref, newest_ref, owner_ref, low_ref, high_ref, delay_ref, out_ref,
    buf, own, packed, head, tiles, before_first, stat_q, fresh, stat_t, means, invs, s1, s2, s3, low, high, delay,
    local_sem, send_sem, recv_sem, z_send, z_recv, q_send, q_recv, t_send, t_recv, halo_send, halo_recv,
):
    me, t = lax.axis_index("band"), lax.axis_index("tm")
    z = me // NQ
    q = me - z * NQ
    barrier = pltpu.get_barrier_semaphore()
    turned = [jnp.where(q + r < NQ, q + r, q + r - NQ) for r in range(NQ)]
    t_peers = [jnp.where(t + i < NT, t + i, t + i - NT) for i in range(1, NT)]
    for i in range(1, NB):
        peer = jnp.where(me + i < NB, me + i, me + i - NB)
        pl.semaphore_signal(barrier, inc=1, device_id={"band": peer}, device_id_type=MESH)
    for k in t_peers:
        pl.semaphore_signal(barrier, inc=1, device_id={"tm": k}, device_id_type=MESH)

    load = pltpu.make_async_copy(newest_ref, fresh, local_sem.at[0])
    load.start()
    last = pltpu.make_async_copy(x_ref.at[:, pl.ds(TILES - 1, 1)], own.at[:, pl.ds(0, 1)], local_sem.at[4])
    last.start()
    tables = [
        pltpu.make_async_copy(src, dst, local_sem.at[1 + i])
        for i, (src, dst) in enumerate(((low_ref, low), (high_ref, high), (delay_ref, delay)))
    ]
    for copy in tables:
        copy.start()

    def spot(c):
        start, size = SPANS[c]
        return x_ref, pl.ds(start, size), pl.ds(FIRST + start, size)

    def send(k, c):
        src, here, there = spot(c)

        def one(peer):
            pltpu.make_async_remote_copy(
                src_ref=src.at[peer, here], dst_ref=buf.at[me, there], send_sem=send_sem.at[c],
                recv_sem=recv_sem.at[c], device_id={"band": peer}, device_id_type=MESH,
            ).start()

        pl.when(k != z)(lambda: one(k * NQ + q))
        for r in range(1, NQ):
            one(k * NQ + turned[r])

    def keep_own(c):
        src, here, there = spot(c)
        pltpu.make_async_copy(src.at[me, here], buf.at[me, there], recv_sem.at[c]).start()

    def arrive(c):
        src, here, there = spot(c)
        pltpu.make_async_copy(src.at[:, here], buf.at[:, there], recv_sem.at[c]).wait()

    for c in range(HEAD):
        keep_own(c)

    row = lax.broadcasted_iota(jnp.int32, (NB, 128), 0)
    column = lax.broadcasted_iota(jnp.int32, (NB, 128), 1)

    def as_row(mean, inv):
        both = jnp.where(column == row, mean, 0.0) + jnp.where(column == row + NB, inv, 0.0)
        return jnp.sum(both, axis=0, keepdims=True)

    def as_columns(stat, first):
        mean = jnp.sum(jnp.where(column == first, stat, 0.0), axis=1, keepdims=True)
        inv = jnp.sum(jnp.where(column == first + NB, stat, 0.0), axis=1, keepdims=True)
        return mean, inv

    load.wait()
    block = fresh[...]
    mean = jnp.sum(jnp.sum(block, axis=1), axis=-1, keepdims=True) * (1.0 / (8 * 128))
    centred = block - mean[:, :, None]
    power = jnp.sum(jnp.sum(centred * centred, axis=1), axis=-1, keepdims=True) * (1.0 / (8 * 128))
    inv = 1.0 / jnp.sqrt(power + 1e-6)
    mine = jnp.where(owner_ref[0] == t, as_row(mean, inv), 0.0)
    last.wait()
    for k in range(NZ):
        packed[k, pl.ds(0, NQ)] = own[pl.ds(k * NQ, NQ), 0, :]
        packed[k, pl.ds(NQ, 1)] = mine
    pl.semaphore_wait(barrier, NB - 1 + NT - 1)

    head_copies = []
    for i in range(1, NZ):
        k = jnp.where(z + i < NZ, z + i, z + i - NZ)
        head_copies.append(pltpu.make_async_remote_copy(
            src_ref=packed.at[k, pl.ds(0, NQ + 1)], dst_ref=head.at[z, pl.ds(0, NQ + 1)], send_sem=z_send,
            recv_sem=z_recv, device_id={"band": k * NQ + q}, device_id_type=MESH,
        ))
        head_copies[-1].start()
    for k, c in PLAN:
        send(k, c)
    head[z, pl.ds(0, NQ + 1)] = packed[z, pl.ds(0, NQ + 1)]

    lane = lax.broadcasted_iota(jnp.int32, (CHUNK, 128), 1)
    sub = lax.broadcasted_iota(jnp.int32, (CHUNK, 128), 0)

    def delayed(high_now, high_before, d):
        return pltpu.roll(jnp.where(lane < 128 - d, high_now, high_before), d, 1)

    def normed(r, where):
        return (buf[r, where] - means[pl.ds(r, 1)]) * invs[pl.ds(r, 1)]

    def pick(level, r):
        half = 2**level
        base = r // (2 * half) * (2 * half)
        return base + low[level, r], base + half + high[level, r]

    def levels(blocks):
        nows = [pl.ds(FIRST + block * CHUNK, CHUNK) for block in blocks]
        befores = [pl.ds(FIRST + block * CHUNK - 1, CHUNK) for block in blocks]
        for even in range(0, NB, 2):
            for block, now, before in zip(blocks, nows, befores):
                base, n_now, n_before = normed(even, now), normed(even + 1, now), normed(even + 1, before)
                if block == 0:
                    n_before = jnp.where((sub > 0) | (t > 0), n_before, 0.0)
                for k in range(2):
                    s1[even + k, now] = base + delayed(n_now, n_before, delay[0, even + k])
        for level, src, dst in ((1, s1, s2), (2, s2, s3), (3, s3, None)):
            for r in range(NB):
                lo, hi = pick(level, r)
                for block, now, before in zip(blocks, nows, befores):
                    value = src[lo, now] + delayed(src[hi, now], src[hi, before], delay[level, r])
                    if dst is None:
                        out_ref[r, pl.ds(block * CHUNK, CHUNK)] = value
                    else:
                        dst[r, now] = value

    def halo_levels():
        tile = pl.ds(FIRST - 1, 1)
        for even in range(0, NB, 2):
            base, over = normed(even, tile), normed(even + 1, tile)
            for k in range(2):
                s1[even + k, tile] = jnp.where(t > 0, base + pltpu.roll(over, delay[0, even + k], 1), 0.0)
        for level, src, dst in ((1, s1, s2), (2, s2, s3)):
            for r in range(NB):
                lo, hi = pick(level, r)
                dst[r, tile] = src[lo, tile] + pltpu.roll(src[hi, tile], delay[level, r], 1)

    landed = head.at[pl.ds(0, NZ - 1), pl.ds(0, NQ + 1)]
    pltpu.make_async_copy(landed, landed, z_recv).wait()
    for r in range(1, NQ):
        there = {"band": z * NQ + turned[r]}
        for i, (src, dst) in enumerate((
            (head.at[:, pl.ds(turned[r], 1)], tiles.at[:, pl.ds(q, 1)]), (head.at[:, pl.ds(NQ, 1)], stat_q.at[:, pl.ds(q, 1)])
        )):
            pltpu.make_async_remote_copy(
                src_ref=src, dst_ref=dst, send_sem=q_send.at[i], recv_sem=q_recv.at[i], device_id=there, device_id_type=MESH
            ).start()
    tiles[:, pl.ds(q, 1)] = head[:, pl.ds(q, 1)]
    stat_q[:, pl.ds(q, 1)] = head[:, pl.ds(NQ, 1)]
    for i, dst in enumerate((tiles, stat_q)):
        part = dst.at[:, pl.ds(0, NQ - 1)]
        pltpu.make_async_copy(part, part, q_recv.at[i]).wait()

    halo = pltpu.make_async_remote_copy(
        src_ref=tiles, dst_ref=before_first, send_sem=halo_send, recv_sem=halo_recv, device_id={"tm": t_peers[0]},
        device_id_type=MESH,
    )
    halo.start()
    stat_t[pl.ds(t, 1)] = as_row(*as_columns(stat_q[...].reshape(NB, 128), me))[None]
    t_copies = []
    for i, k in enumerate(t_peers):
        t_copies.append(pltpu.make_async_remote_copy(
            src_ref=stat_t.at[t], dst_ref=stat_t.at[t], send_sem=t_send.at[i], recv_sem=t_recv.at[i],
            device_id={"tm": k}, device_id_type=MESH,
        ))
        t_copies[-1].start()
    for copy in t_copies:
        copy.wait_recv()
    stat = stat_t[0]
    for i in range(1, NT):
        stat = stat + stat_t[i]
    mean, inv = as_columns(stat, row)
    means[...] = jnp.broadcast_to(mean, (NB, 128))
    invs[...] = jnp.broadcast_to(inv, (NB, 128))
    for copy in tables:
        copy.wait()
    halo.wait_recv()
    buf[:, FIRST - 1, :] = before_first[...].reshape(NB, 128)
    buf[:, ROWS - 1, :] = tiles[...].reshape(NB, 128)
    halo_levels()
    for c, (start, size) in enumerate(SPANS):
        arrive(c)
        levels(range(start // CHUNK, (start + size + 1) // CHUNK))

    halo.wait_send()
    for copy in t_copies:
        copy.wait_send()
    pltpu.make_async_copy(landed, landed, z_send).wait()
    for i, dst in enumerate((tiles, stat_q)):
        part = dst.at[:, pl.ds(0, NQ - 1)]
        pltpu.make_async_copy(part, part, q_send.at[i]).wait()
    for c in range(HEAD):
        src, here, there = spot(c)
        sent, landed = src.at[pl.ds(0, NB - 1), here], buf.at[pl.ds(0, NB - 1), there]
        pltpu.make_async_copy(sent, landed, send_sem.at[c]).wait()


def shards(spectra, newest, ingest_owner, low_trial, high_trial, delay_table):
    operands = [spectra.reshape(NB, TILES, 128), newest.reshape(NB, 8, 128)]
    operands += [ingest_owner, low_trial, high_trial, delay_table]
    operands = [a if a.size == 1 else pltpu.with_memory_space_constraint(a, pltpu.HBM) for a in operands]
    state = pltpu.VMEM((NB, ROWS, 128), jnp.float32)
    table = pltpu.SMEM((LEVELS, NB), jnp.int32)
    many = pltpu.SemaphoreType.DMA((HEAD,))
    square = pltpu.VMEM((NZ, NQ, 128), jnp.float32)
    out = pl.pallas_call(
        kernel,
        out_shape=jax.ShapeDtypeStruct((NB, TILES, 128), jnp.float32),
        in_specs=[pl.BlockSpec(memory_space=pltpu.SMEM if a.size == 1 else pl.ANY) for a in operands],
        out_specs=pl.BlockSpec(memory_space=pltpu.VMEM),
        scratch_shapes=[
            state,
            pltpu.VMEM((NB, 8, 128), jnp.float32),
            pltpu.VMEM((NZ, 2 * NQ, 128), jnp.float32),
            pltpu.VMEM((NZ, 2 * NQ, 128), jnp.float32),
            square, square, square,
            pltpu.VMEM((NB, 8, 128), jnp.float32),
            pltpu.VMEM((NT, 1, 128), jnp.float32),
            pltpu.VMEM((NB, 128), jnp.float32),
            pltpu.VMEM((NB, 128), jnp.float32),
            state, state, state,
            table, table, table,
            pltpu.SemaphoreType.DMA((5,)),
            many, many,
            pltpu.SemaphoreType.DMA,
            pltpu.SemaphoreType.DMA,
            pltpu.SemaphoreType.DMA((2,)),
            pltpu.SemaphoreType.DMA((2,)),
            pltpu.SemaphoreType.DMA((NT - 1,)),
            pltpu.SemaphoreType.DMA((NT - 1,)),
            pltpu.SemaphoreType.DMA,
            pltpu.SemaphoreType.DMA,
        ],
        compiler_params=pltpu.CompilerParams(collective_id=1, has_side_effects=True, vmem_limit_bytes=24 << 20),
    )(*operands)
    return out.reshape(NB // 16, 16, TILES * 128)


def solution(mesh):
    return jax.shard_map(
        shards,
        mesh=mesh,
        in_specs=(
            P(None, "band", "tm"),
            P(None, "band", "tm", None),
            P("band"),
            P(None, "band"),
            P(None, "band"),
            P(None, "band"),
        ),
        out_specs=P("band", None, "tm"),
        check_vma=False,
    )
```

```python
import functools

import jax
import jax.numpy as jnp
from jax import lax
from jax.experimental import pallas as pl
from jax.experimental.pallas import tpu as pltpu
from jax.sharding import PartitionSpec as P

LEVELS = 4
NB, NT = 64, 4
NZ, NQ = 8, 8
TILES = 32
CHUNK = 8
FIRST = 8
ROWS = FIRST + TILES
BODY = TILES - 1
GROUPS = 4
ALL = tuple(range(NQ))
PLAN = [(0, ALL), (1, ALL[:6]), (2, ALL[:7]), (1, ALL[6:]), (2, ALL[7:])] + [(k, ALL) for k in (3, 7, 6, 5, 4)]
MESH = pl.DeviceIdType.MESH


def kernel(
    x_ref, newest_ref, owner_ref, low_ref, high_ref, delay_ref, out_ref,
    buf, own, packed, head, tiles, before_first, stat_q, fresh, stat_t, means, invs, s1, s2, s3, low, high, delay,
    local_sem, send_sem, recv_sem, z_send, z_recv, q_send, q_recv, t_send, t_recv, halo_send, halo_recv,
):
    me, t = lax.axis_index("band"), lax.axis_index("tm")
    z = me // NQ
    q = me - z * NQ
    barrier = pltpu.get_barrier_semaphore()
    turned = [jnp.where(q + r < NQ, q + r, q + r - NQ) for r in range(NQ)]
    t_peers = [jnp.where(t + i < NT, t + i, t + i - NT) for i in range(1, NT)]
    for i in range(1, NB):
        peer = jnp.where(me + i < NB, me + i, me + i - NB)
        pl.semaphore_signal(barrier, inc=1, device_id={"band": peer}, device_id_type=MESH)
    for k in t_peers:
        pl.semaphore_signal(barrier, inc=1, device_id={"tm": k}, device_id_type=MESH)

    load = pltpu.make_async_copy(newest_ref, fresh, local_sem.at[0])
    load.start()
    last = pltpu.make_async_copy(x_ref.at[:, pl.ds(TILES - 1, 1)], own.at[:, pl.ds(0, 1)], local_sem.at[4])
    last.start()
    tables = [
        pltpu.make_async_copy(src, dst, local_sem.at[1 + i])
        for i, (src, dst) in enumerate(((low_ref, low), (high_ref, high), (delay_ref, delay)))
    ]
    for copy in tables:
        copy.start()

    def send(k, turns):
        def one(peer):
            pltpu.make_async_remote_copy(
                src_ref=x_ref.at[peer, pl.ds(0, BODY)], dst_ref=buf.at[me, pl.ds(FIRST, BODY)], send_sem=send_sem,
                recv_sem=recv_sem.at[z // 2], device_id={"band": peer}, device_id_type=MESH,
            ).start()

        for r in turns:
            if r == 0:
                pl.when(k != z)(lambda: one(k * NQ + q))
            else:
                one(k * NQ + turned[r])

    def arrive(g):
        rows = buf.at[pl.ds(g * 16, 16), pl.ds(FIRST, BODY)]
        pltpu.make_async_copy(rows, rows, recv_sem.at[g]).wait()

    pltpu.make_async_copy(x_ref.at[me, pl.ds(0, BODY)], buf.at[me, pl.ds(FIRST, BODY)], recv_sem.at[z // 2]).start()

    row = lax.broadcasted_iota(jnp.int32, (NB, 128), 0)
    column = lax.broadcasted_iota(jnp.int32, (NB, 128), 1)

    def as_row(mean, inv):
        both = jnp.where(column == row, mean, 0.0) + jnp.where(column == row + NB, inv, 0.0)
        return jnp.sum(both, axis=0, keepdims=True)

    def as_columns(stat, first):
        mean = jnp.sum(jnp.where(column == first, stat, 0.0), axis=1, keepdims=True)
        inv = jnp.sum(jnp.where(column == first + NB, stat, 0.0), axis=1, keepdims=True)
        return mean, inv

    load.wait()
    block = fresh[...]
    mean = jnp.sum(jnp.sum(block, axis=1), axis=-1, keepdims=True) * (1.0 / (8 * 128))
    centred = block - mean[:, :, None]
    power = jnp.sum(jnp.sum(centred * centred, axis=1), axis=-1, keepdims=True) * (1.0 / (8 * 128))
    inv = 1.0 / jnp.sqrt(power + 1e-6)
    mine = jnp.where(owner_ref[0] == t, as_row(mean, inv), 0.0)
    last.wait()
    for k in range(NZ):
        packed[k, pl.ds(0, NQ)] = own[pl.ds(k * NQ, NQ), 0, :]
        packed[k, pl.ds(NQ, 1)] = mine
    pl.semaphore_wait(barrier, NB - 1 + NT - 1)

    head_copies = []
    for i in range(1, NZ):
        k = jnp.where(z + i < NZ, z + i, z + i - NZ)
        head_copies.append(pltpu.make_async_remote_copy(
            src_ref=packed.at[k, pl.ds(0, NQ + 1)], dst_ref=head.at[z, pl.ds(0, NQ + 1)], send_sem=z_send,
            recv_sem=z_recv, device_id={"band": k * NQ + q}, device_id_type=MESH,
        ))
        head_copies[-1].start()
    for k, turns in PLAN:
        send(k, turns)
    head[z, pl.ds(0, NQ + 1)] = packed[z, pl.ds(0, NQ + 1)]

    lane = lax.broadcasted_iota(jnp.int32, (CHUNK, 128), 1)
    sub = lax.broadcasted_iota(jnp.int32, (CHUNK, 128), 0)

    def delayed(high_now, high_before, d):
        return pltpu.roll(jnp.where(lane < 128 - d, high_now, high_before), d, 1)

    def normed(r, where):
        return (buf[r, where] - means[pl.ds(r, 1)]) * invs[pl.ds(r, 1)]

    def pick(level, r):
        half = 2**level
        base = r // (2 * half) * (2 * half)
        return base + low[level, r], base + half + high[level, r]

    blocks = range(TILES // CHUNK)
    nows = [pl.ds(FIRST + block * CHUNK, CHUNK) for block in blocks]
    befores = [pl.ds(FIRST + block * CHUNK - 1, CHUNK) for block in blocks]

    def levels(g):
        for even in range(g * 16, g * 16 + 16, 2):
            for block, now, before in zip(blocks, nows, befores):
                base, n_now, n_before = normed(even, now), normed(even + 1, now), normed(even + 1, before)
                if block == 0:
                    n_before = jnp.where((sub > 0) | (t > 0), n_before, 0.0)
                for k in range(2):
                    s1[even + k, now] = base + delayed(n_now, n_before, delay[0, even + k])
        for level, src, dst in ((1, s1, s2), (2, s2, s3), (3, s3, None)):
            for r in range(g * 16, g * 16 + 16):
                lo, hi = pick(level, r)
                for block, now, before in zip(blocks, nows, befores):
                    value = src[lo, now] + delayed(src[hi, now], src[hi, before], delay[level, r])
                    if dst is None:
                        out_ref[r, pl.ds(block * CHUNK, CHUNK)] = value
                    else:
                        dst[r, now] = value

    def halo_levels():
        tile = pl.ds(FIRST - 1, 1)
        for even in range(0, NB, 2):
            base, over = normed(even, tile), normed(even + 1, tile)
            for k in range(2):
                s1[even + k, tile] = jnp.where(t > 0, base + pltpu.roll(over, delay[0, even + k], 1), 0.0)
        for level, src, dst in ((1, s1, s2), (2, s2, s3)):
            for r in range(NB):
                lo, hi = pick(level, r)
                dst[r, tile] = src[lo, tile] + pltpu.roll(src[hi, tile], delay[level, r], 1)

    landed = head.at[pl.ds(0, NZ - 1), pl.ds(0, NQ + 1)]
    pltpu.make_async_copy(landed, landed, z_recv).wait()
    for r in range(1, NQ):
        there = {"band": z * NQ + turned[r]}
        for i, (src, dst) in enumerate((
            (head.at[:, pl.ds(turned[r], 1)], tiles.at[:, pl.ds(q, 1)]), (head.at[:, pl.ds(NQ, 1)], stat_q.at[:, pl.ds(q, 1)])
        )):
            pltpu.make_async_remote_copy(
                src_ref=src, dst_ref=dst, send_sem=q_send.at[i], recv_sem=q_recv.at[i], device_id=there, device_id_type=MESH
            ).start()
    tiles[:, pl.ds(q, 1)] = head[:, pl.ds(q, 1)]
    stat_q[:, pl.ds(q, 1)] = head[:, pl.ds(NQ, 1)]
    for i, dst in enumerate((tiles, stat_q)):
        part = dst.at[:, pl.ds(0, NQ - 1)]
        pltpu.make_async_copy(part, part, q_recv.at[i]).wait()

    halo = pltpu.make_async_remote_copy(
        src_ref=tiles, dst_ref=before_first, send_sem=halo_send, recv_sem=halo_recv, device_id={"tm": t_peers[0]},
        device_id_type=MESH,
    )
    halo.start()
    stat_t[pl.ds(t, 1)] = as_row(*as_columns(stat_q[...].reshape(NB, 128), me))[None]
    t_copies = []
    for i, k in enumerate(t_peers):
        t_copies.append(pltpu.make_async_remote_copy(
            src_ref=stat_t.at[t], dst_ref=stat_t.at[t], send_sem=t_send.at[i], recv_sem=t_recv.at[i],
            device_id={"tm": k}, device_id_type=MESH,
        ))
        t_copies[-1].start()
    for copy in t_copies:
        copy.wait_recv()
    stat = stat_t[0]
    for i in range(1, NT):
        stat = stat + stat_t[i]
    mean, inv = as_columns(stat, row)
    means[...] = jnp.broadcast_to(mean, (NB, 128))
    invs[...] = jnp.broadcast_to(inv, (NB, 128))
    for copy in tables:
        copy.wait()
    halo.wait_recv()
    buf[:, FIRST - 1, :] = before_first[...].reshape(NB, 128)
    buf[:, ROWS - 1, :] = tiles[...].reshape(NB, 128)
    halo_levels()
    def merge(order):
        for g in order:
            arrive(g)
            levels(g)

    far_last = (z < NZ // 2) | (z == 5)
    pl.when(far_last)(lambda: merge((0, 1, 2, 3)))
    pl.when(jnp.logical_not(far_last))(lambda: merge((3, 2, 0, 1)))

    halo.wait_send()
    for copy in t_copies:
        copy.wait_send()
    pltpu.make_async_copy(landed, landed, z_send).wait()
    for i, dst in enumerate((tiles, stat_q)):
        part = dst.at[:, pl.ds(0, NQ - 1)]
        pltpu.make_async_copy(part, part, q_send.at[i]).wait()
    rows = buf.at[pl.ds(0, NB - 1), pl.ds(FIRST, BODY)]
    pltpu.make_async_copy(rows, rows, send_sem).wait()


def shards(spectra, newest, ingest_owner, low_trial, high_trial, delay_table):
    operands = [spectra.reshape(NB, TILES, 128), newest.reshape(NB, 8, 128)]
    operands += [ingest_owner, low_trial, high_trial, delay_table]
    operands = [a if a.size == 1 else pltpu.with_memory_space_constraint(a, pltpu.HBM) for a in operands]
    state = pltpu.VMEM((NB, ROWS, 128), jnp.float32)
    table = pltpu.SMEM((LEVELS, NB), jnp.int32)
    square = pltpu.VMEM((NZ, NQ, 128), jnp.float32)
    out = pl.pallas_call(
        kernel,
        out_shape=jax.ShapeDtypeStruct((NB, TILES, 128), jnp.float32),
        in_specs=[pl.BlockSpec(memory_space=pltpu.SMEM if a.size == 1 else pl.ANY) for a in operands],
        out_specs=pl.BlockSpec(memory_space=pltpu.VMEM),
        scratch_shapes=[
            state,
            pltpu.VMEM((NB, 8, 128), jnp.float32),
            pltpu.VMEM((NZ, 2 * NQ, 128), jnp.float32),
            pltpu.VMEM((NZ, 2 * NQ, 128), jnp.float32),
            square, square, square,
            pltpu.VMEM((NB, 8, 128), jnp.float32),
            pltpu.VMEM((NT, 1, 128), jnp.float32),
            pltpu.VMEM((NB, 128), jnp.float32),
            pltpu.VMEM((NB, 128), jnp.float32),
            state, state, state,
            table, table, table,
            pltpu.SemaphoreType.DMA((5,)),
            pltpu.SemaphoreType.DMA,
            pltpu.SemaphoreType.DMA((GROUPS,)),
            pltpu.SemaphoreType.DMA,
            pltpu.SemaphoreType.DMA,
            pltpu.SemaphoreType.DMA((2,)),
            pltpu.SemaphoreType.DMA((2,)),
            pltpu.SemaphoreType.DMA((NT - 1,)),
            pltpu.SemaphoreType.DMA((NT - 1,)),
            pltpu.SemaphoreType.DMA,
            pltpu.SemaphoreType.DMA,
        ],
        compiler_params=pltpu.CompilerParams(collective_id=1, has_side_effects=True, vmem_limit_bytes=24 << 20),
    )(*operands)
    return out.reshape(NB // 16, 16, TILES * 128)


def solution(mesh):
    return jax.shard_map(
        shards,
        mesh=mesh,
        in_specs=(
            P(None, "band", "tm"),
            P(None, "band", "tm", None),
            P("band"),
            P(None, "band"),
            P(None, "band"),
            P(None, "band"),
        ),
        out_specs=P("band", None, "tm"),
        check_vma=False,
    )
```

```python
import functools

import jax
import jax.numpy as jnp
from jax import lax
from jax.experimental import pallas as pl
from jax.experimental.pallas import tpu as pltpu
from jax.sharding import PartitionSpec as P

LEVELS = 4
NB, NT = 64, 4
NZ, NQ = 8, 8
TILES = 32
CHUNK = 8
FIRST = 8
ROWS = FIRST + TILES
BODY = TILES - 1
GROUPS = 4
ALL = tuple(range(NQ))
PLAN = [(0, ALL), (1, ALL[:6]), (2, ALL[:7]), (1, ALL[6:]), (2, ALL[7:])] + [(k, ALL) for k in (3, 7, 6, 5, 4)]
MESH = pl.DeviceIdType.MESH


def kernel(
    x_ref, newest_ref, owner_ref, low_ref, high_ref, delay_ref, out_ref,
    buf, own, packed, head, tiles, before_first, stat_q, fresh, stat_t, means, invs, s1, s2, s3, low, high, delay,
    local_sem, send_sem, recv_sem, z_send, z_recv, q_send, q_recv, t_send, t_recv, halo_send, halo_recv,
):
    me, t = lax.axis_index("band"), lax.axis_index("tm")
    z = me // NQ
    q = me - z * NQ
    barrier = pltpu.get_barrier_semaphore()
    turned = [jnp.where(q + r < NQ, q + r, q + r - NQ) for r in range(NQ)]
    t_peers = [jnp.where(t + i < NT, t + i, t + i - NT) for i in range(1, NT)]
    for i in sorted(range(1, NB), key=lambda i: abs(i - NB // 2)):
        peer = jnp.where(me + i < NB, me + i, me + i - NB)
        pl.semaphore_signal(barrier, inc=1, device_id={"band": peer}, device_id_type=MESH)
    for k in t_peers:
        pl.semaphore_signal(barrier, inc=1, device_id={"tm": k}, device_id_type=MESH)

    load = pltpu.make_async_copy(newest_ref, fresh, local_sem.at[0])
    load.start()
    last = pltpu.make_async_copy(x_ref.at[:, pl.ds(TILES - 1, 1)], own.at[:, pl.ds(0, 1)], local_sem.at[4])
    last.start()
    tables = [
        pltpu.make_async_copy(src, dst, local_sem.at[1 + i])
        for i, (src, dst) in enumerate(((low_ref, low), (high_ref, high), (delay_ref, delay)))
    ]
    for copy in tables:
        copy.start()

    def send(k, turns):
        def one(peer):
            pltpu.make_async_remote_copy(
                src_ref=x_ref.at[peer, pl.ds(0, BODY)], dst_ref=buf.at[me, pl.ds(FIRST, BODY)], send_sem=send_sem,
                recv_sem=recv_sem.at[z // 2], device_id={"band": peer}, device_id_type=MESH,
            ).start()

        for r in turns:
            if r == 0:
                pl.when(k != z)(lambda: one(k * NQ + q))
            else:
                one(k * NQ + turned[r])

    def arrive(g):
        rows = buf.at[pl.ds(g * 16, 16), pl.ds(FIRST, BODY)]
        pltpu.make_async_copy(rows, rows, recv_sem.at[g]).wait()

    pltpu.make_async_copy(x_ref.at[me, pl.ds(0, BODY)], buf.at[me, pl.ds(FIRST, BODY)], recv_sem.at[z // 2]).start()

    row = lax.broadcasted_iota(jnp.int32, (NB, 128), 0)
    column = lax.broadcasted_iota(jnp.int32, (NB, 128), 1)

    def as_row(mean, inv):
        both = jnp.where(column == row, mean, 0.0) + jnp.where(column == row + NB, inv, 0.0)
        return jnp.sum(both, axis=0, keepdims=True)

    def as_columns(stat, first):
        mean = jnp.sum(jnp.where(column == first, stat, 0.0), axis=1, keepdims=True)
        inv = jnp.sum(jnp.where(column == first + NB, stat, 0.0), axis=1, keepdims=True)
        return mean, inv

    load.wait()
    block = fresh[...]
    mean = jnp.sum(jnp.sum(block, axis=1), axis=-1, keepdims=True) * (1.0 / (8 * 128))
    centred = block - mean[:, :, None]
    power = jnp.sum(jnp.sum(centred * centred, axis=1), axis=-1, keepdims=True) * (1.0 / (8 * 128))
    inv = 1.0 / jnp.sqrt(power + 1e-6)
    mine = jnp.where(owner_ref[0] == t, as_row(mean, inv), 0.0)
    last.wait()
    for k in range(NZ):
        packed[k, pl.ds(0, NQ)] = own[pl.ds(k * NQ, NQ), 0, :]
        packed[k, pl.ds(NQ, 1)] = mine
    pl.semaphore_wait(barrier, NB - 1 + NT - 1)

    head_copies = []
    for i in range(1, NZ):
        k = jnp.where(z + i < NZ, z + i, z + i - NZ)
        head_copies.append(pltpu.make_async_remote_copy(
            src_ref=packed.at[k, pl.ds(0, NQ + 1)], dst_ref=head.at[z, pl.ds(0, NQ + 1)], send_sem=z_send,
            recv_sem=z_recv, device_id={"band": k * NQ + q}, device_id_type=MESH,
        ))
        head_copies[-1].start()
    for k, turns in PLAN:
        send(k, turns)
    head[z, pl.ds(0, NQ + 1)] = packed[z, pl.ds(0, NQ + 1)]

    lane = lax.broadcasted_iota(jnp.int32, (CHUNK, 128), 1)
    sub = lax.broadcasted_iota(jnp.int32, (CHUNK, 128), 0)

    def delayed(high_now, high_before, d):
        return pltpu.roll(jnp.where(lane < 128 - d, high_now, high_before), d, 1)

    def normed(r, where):
        return (buf[r, where] - means[pl.ds(r, 1)]) * invs[pl.ds(r, 1)]

    def pick(level, r):
        half = 2**level
        base = r // (2 * half) * (2 * half)
        return base + low[level, r], base + half + high[level, r]

    blocks = range(TILES // CHUNK)
    nows = [pl.ds(FIRST + block * CHUNK, CHUNK) for block in blocks]
    befores = [pl.ds(FIRST + block * CHUNK - 1, CHUNK) for block in blocks]

    def levels(g):
        for even in range(g * 16, g * 16 + 16, 2):
            for block, now, before in zip(blocks, nows, befores):
                base, n_now, n_before = normed(even, now), normed(even + 1, now), normed(even + 1, before)
                if block == 0:
                    n_before = jnp.where((sub > 0) | (t > 0), n_before, 0.0)
                for k in range(2):
                    s1[even + k, now] = base + delayed(n_now, n_before, delay[0, even + k])
        for level, src, dst in ((1, s1, s2), (2, s2, s3), (3, s3, None)):
            for r in range(g * 16, g * 16 + 16):
                lo, hi = pick(level, r)
                for block, now, before in zip(blocks, nows, befores):
                    value = src[lo, now] + delayed(src[hi, now], src[hi, before], delay[level, r])
                    if dst is None:
                        out_ref[r, pl.ds(block * CHUNK, CHUNK)] = value
                    else:
                        dst[r, now] = value

    def halo_levels():
        tile = pl.ds(FIRST - 1, 1)
        for even in range(0, NB, 2):
            base, over = normed(even, tile), normed(even + 1, tile)
            for k in range(2):
                s1[even + k, tile] = jnp.where(t > 0, base + pltpu.roll(over, delay[0, even + k], 1), 0.0)
        for level, src, dst in ((1, s1, s2), (2, s2, s3)):
            for r in range(NB):
                lo, hi = pick(level, r)
                dst[r, tile] = src[lo, tile] + pltpu.roll(src[hi, tile], delay[level, r], 1)

    landed = head.at[pl.ds(0, NZ - 1), pl.ds(0, NQ + 1)]
    pltpu.make_async_copy(landed, landed, z_recv).wait()
    for r in range(1, NQ):
        there = {"band": z * NQ + turned[r]}
        for i, (src, dst) in enumerate((
            (head.at[:, pl.ds(turned[r], 1)], tiles.at[:, pl.ds(q, 1)]), (head.at[:, pl.ds(NQ, 1)], stat_q.at[:, pl.ds(q, 1)])
        )):
            pltpu.make_async_remote_copy(
                src_ref=src, dst_ref=dst, send_sem=q_send.at[i], recv_sem=q_recv.at[i], device_id=there, device_id_type=MESH
            ).start()
    tiles[:, pl.ds(q, 1)] = head[:, pl.ds(q, 1)]
    stat_q[:, pl.ds(q, 1)] = head[:, pl.ds(NQ, 1)]
    for i, dst in enumerate((tiles, stat_q)):
        part = dst.at[:, pl.ds(0, NQ - 1)]
        pltpu.make_async_copy(part, part, q_recv.at[i]).wait()

    halo = pltpu.make_async_remote_copy(
        src_ref=tiles, dst_ref=before_first, send_sem=halo_send, recv_sem=halo_recv, device_id={"tm": t_peers[0]},
        device_id_type=MESH,
    )
    halo.start()
    stat_t[pl.ds(t, 1)] = as_row(*as_columns(stat_q[...].reshape(NB, 128), me))[None]
    t_copies = []
    for i, k in enumerate(t_peers):
        t_copies.append(pltpu.make_async_remote_copy(
            src_ref=stat_t.at[t], dst_ref=stat_t.at[t], send_sem=t_send.at[i], recv_sem=t_recv.at[i],
            device_id={"tm": k}, device_id_type=MESH,
        ))
        t_copies[-1].start()
    for copy in t_copies:
        copy.wait_recv()
    stat = stat_t[0]
    for i in range(1, NT):
        stat = stat + stat_t[i]
    mean, inv = as_columns(stat, row)
    means[...] = jnp.broadcast_to(mean, (NB, 128))
    invs[...] = jnp.broadcast_to(inv, (NB, 128))
    for copy in tables:
        copy.wait()
    halo.wait_recv()
    buf[:, FIRST - 1, :] = before_first[...].reshape(NB, 128)
    buf[:, ROWS - 1, :] = tiles[...].reshape(NB, 128)
    halo_levels()
    def settle():
        halo.wait_send()
        for copy in t_copies:
            copy.wait_send()
        pltpu.make_async_copy(landed, landed, z_send).wait()
        for i, dst in enumerate((tiles, stat_q)):
            part = dst.at[:, pl.ds(0, NQ - 1)]
            pltpu.make_async_copy(part, part, q_send.at[i]).wait()

    def merge(order):
        for g in order:
            if g == order[-1]:
                settle()
            arrive(g)
            levels(g)

    far_last = (z < NZ // 2) | (z == 5)
    pl.when(far_last)(lambda: merge((0, 1, 2, 3)))
    pl.when(jnp.logical_not(far_last))(lambda: merge((3, 2, 0, 1)))

    rows = buf.at[pl.ds(0, NB - 1), pl.ds(FIRST, BODY)]
    pltpu.make_async_copy(rows, rows, send_sem).wait()


def shards(spectra, newest, ingest_owner, low_trial, high_trial, delay_table):
    operands = [spectra.reshape(NB, TILES, 128), newest.reshape(NB, 8, 128)]
    operands += [ingest_owner, low_trial, high_trial, delay_table]
    operands = [a if a.size == 1 else pltpu.with_memory_space_constraint(a, pltpu.HBM) for a in operands]
    state = pltpu.VMEM((NB, ROWS, 128), jnp.float32)
    table = pltpu.SMEM((LEVELS, NB), jnp.int32)
    square = pltpu.VMEM((NZ, NQ, 128), jnp.float32)
    out = pl.pallas_call(
        kernel,
        out_shape=jax.ShapeDtypeStruct((NB, TILES, 128), jnp.float32),
        in_specs=[pl.BlockSpec(memory_space=pltpu.SMEM if a.size == 1 else pl.ANY) for a in operands],
        out_specs=pl.BlockSpec(memory_space=pltpu.VMEM),
        scratch_shapes=[
            state,
            pltpu.VMEM((NB, 8, 128), jnp.float32),
            pltpu.VMEM((NZ, 2 * NQ, 128), jnp.float32),
            pltpu.VMEM((NZ, 2 * NQ, 128), jnp.float32),
            square, square, square,
            pltpu.VMEM((NB, 8, 128), jnp.float32),
            pltpu.VMEM((NT, 1, 128), jnp.float32),
            pltpu.VMEM((NB, 128), jnp.float32),
            pltpu.VMEM((NB, 128), jnp.float32),
            state, state, state,
            table, table, table,
            pltpu.SemaphoreType.DMA((5,)),
            pltpu.SemaphoreType.DMA,
            pltpu.SemaphoreType.DMA((GROUPS,)),
            pltpu.SemaphoreType.DMA,
            pltpu.SemaphoreType.DMA,
            pltpu.SemaphoreType.DMA((2,)),
            pltpu.SemaphoreType.DMA((2,)),
            pltpu.SemaphoreType.DMA((NT - 1,)),
            pltpu.SemaphoreType.DMA((NT - 1,)),
            pltpu.SemaphoreType.DMA,
            pltpu.SemaphoreType.DMA,
        ],
        compiler_params=pltpu.CompilerParams(collective_id=1, has_side_effects=True, vmem_limit_bytes=24 << 20),
    )(*operands)
    return out.reshape(NB // 16, 16, TILES * 128)


def solution(mesh):
    return jax.shard_map(
        shards,
        mesh=mesh,
        in_specs=(
            P(None, "band", "tm"),
            P(None, "band", "tm", None),
            P("band"),
            P(None, "band"),
            P(None, "band"),
            P(None, "band"),
        ),
        out_specs=P("band", None, "tm"),
        check_vma=False,
    )
```

```python
import functools

import jax
import jax.numpy as jnp
from jax import lax
from jax.experimental import pallas as pl
from jax.experimental.pallas import tpu as pltpu
from jax.sharding import PartitionSpec as P

LEVELS = 4
NB, NT = 64, 4
NZ, NQ = 8, 8
TILES = 32
CHUNK = 8
FIRST = 8
ROWS = FIRST + TILES
BODY = TILES - 1
GROUPS = 4
ALL = (4, 5, 2, 3, 6, 7, 0, 1)
PLAN = [(0, ALL), (1, ALL), (2, ALL)] + [(k, ALL) for k in (3, 7, 6, 5, 4)]
MESH = pl.DeviceIdType.MESH


def kernel(
    x_ref, newest_ref, owner_ref, low_ref, high_ref, delay_ref, out_ref,
    buf, own, packed, head, tiles, before_first, stat_q, fresh, stat_t, means, invs, s1, s2, s3, low, high, delay,
    local_sem, send_sem, recv_sem, z_send, z_recv, q_send, q_recv, t_send, t_recv, halo_send, halo_recv,
):
    me, t = lax.axis_index("band"), lax.axis_index("tm")
    z = me // NQ
    q = me - z * NQ
    barrier = pltpu.get_barrier_semaphore()
    turned = [jnp.where(q + r < NQ, q + r, q + r - NQ) for r in range(NQ)]
    t_peers = [jnp.where(t + i < NT, t + i, t + i - NT) for i in range(1, NT)]
    for i in sorted(range(1, NB), key=lambda i: abs(i - NB // 2)):
        peer = jnp.where(me + i < NB, me + i, me + i - NB)
        pl.semaphore_signal(barrier, inc=1, device_id={"band": peer}, device_id_type=MESH)
    for k in t_peers:
        pl.semaphore_signal(barrier, inc=1, device_id={"tm": k}, device_id_type=MESH)

    load = pltpu.make_async_copy(newest_ref, fresh, local_sem.at[0])
    load.start()
    last = pltpu.make_async_copy(x_ref.at[:, pl.ds(TILES - 1, 1)], own.at[:, pl.ds(0, 1)], local_sem.at[4])
    last.start()
    tables = [
        pltpu.make_async_copy(src, dst, local_sem.at[1 + i])
        for i, (src, dst) in enumerate(((low_ref, low), (high_ref, high), (delay_ref, delay)))
    ]
    for copy in tables:
        copy.start()

    def send(k, turns):
        def one(peer):
            pltpu.make_async_remote_copy(
                src_ref=x_ref.at[peer, pl.ds(0, BODY)], dst_ref=buf.at[me, pl.ds(FIRST, BODY)], send_sem=send_sem,
                recv_sem=recv_sem.at[z // 2], device_id={"band": peer}, device_id_type=MESH,
            ).start()

        for r in turns:
            if r == 0:
                pl.when(k != z)(lambda: one(k * NQ + q))
            else:
                one(k * NQ + turned[r])

    def arrive(g):
        rows = buf.at[pl.ds(g * 16, 16), pl.ds(FIRST, BODY)]
        pltpu.make_async_copy(rows, rows, recv_sem.at[g]).wait()

    pltpu.make_async_copy(x_ref.at[me, pl.ds(0, BODY)], buf.at[me, pl.ds(FIRST, BODY)], recv_sem.at[z // 2]).start()

    row = lax.broadcasted_iota(jnp.int32, (NB, 128), 0)
    column = lax.broadcasted_iota(jnp.int32, (NB, 128), 1)

    def as_row(mean, inv):
        both = jnp.where(column == row, mean, 0.0) + jnp.where(column == row + NB, inv, 0.0)
        return jnp.sum(both, axis=0, keepdims=True)

    def as_columns(stat, first):
        mean = jnp.sum(jnp.where(column == first, stat, 0.0), axis=1, keepdims=True)
        inv = jnp.sum(jnp.where(column == first + NB, stat, 0.0), axis=1, keepdims=True)
        return mean, inv

    load.wait()
    block = fresh[...]
    mean = jnp.sum(jnp.sum(block, axis=1), axis=-1, keepdims=True) * (1.0 / (8 * 128))
    centred = block - mean[:, :, None]
    power = jnp.sum(jnp.sum(centred * centred, axis=1), axis=-1, keepdims=True) * (1.0 / (8 * 128))
    inv = 1.0 / jnp.sqrt(power + 1e-6)
    mine = jnp.where(owner_ref[0] == t, as_row(mean, inv), 0.0)
    last.wait()
    for k in range(NZ):
        packed[k, pl.ds(0, NQ)] = own[pl.ds(k * NQ, NQ), 0, :]
        packed[k, pl.ds(NQ, 1)] = mine
    pl.semaphore_wait(barrier, NB - 1 + NT - 1)

    head_copies = []
    for i in range(1, NZ):
        k = jnp.where(z + i < NZ, z + i, z + i - NZ)
        head_copies.append(pltpu.make_async_remote_copy(
            src_ref=packed.at[k, pl.ds(0, NQ + 1)], dst_ref=head.at[z, pl.ds(0, NQ + 1)], send_sem=z_send,
            recv_sem=z_recv, device_id={"band": k * NQ + q}, device_id_type=MESH,
        ))
        head_copies[-1].start()
    for k, turns in PLAN:
        send(k, turns)
    head[z, pl.ds(0, NQ + 1)] = packed[z, pl.ds(0, NQ + 1)]

    lane = lax.broadcasted_iota(jnp.int32, (CHUNK, 128), 1)
    sub = lax.broadcasted_iota(jnp.int32, (CHUNK, 128), 0)

    def delayed(high_now, high_before, d):
        return pltpu.roll(jnp.where(lane < 128 - d, high_now, high_before), d, 1)

    def normed(r, where):
        return (buf[r, where] - means[pl.ds(r, 1)]) * invs[pl.ds(r, 1)]

    def pick(level, r):
        half = 2**level
        base = r // (2 * half) * (2 * half)
        return base + low[level, r], base + half + high[level, r]

    blocks = range(TILES // CHUNK)
    nows = [pl.ds(FIRST + block * CHUNK, CHUNK) for block in blocks]
    befores = [pl.ds(FIRST + block * CHUNK - 1, CHUNK) for block in blocks]

    def levels(g):
        for even in range(g * 16, g * 16 + 16, 2):
            for block, now, before in zip(blocks, nows, befores):
                base, n_now, n_before = normed(even, now), normed(even + 1, now), normed(even + 1, before)
                if block == 0:
                    n_before = jnp.where((sub > 0) | (t > 0), n_before, 0.0)
                for k in range(2):
                    s1[even + k, now] = base + delayed(n_now, n_before, delay[0, even + k])
        for level, src, dst in ((1, s1, s2), (2, s2, s3), (3, s3, None)):
            for r in range(g * 16, g * 16 + 16):
                lo, hi = pick(level, r)
                for block, now, before in zip(blocks, nows, befores):
                    value = src[lo, now] + delayed(src[hi, now], src[hi, before], delay[level, r])
                    if dst is None:
                        out_ref[r, pl.ds(block * CHUNK, CHUNK)] = value
                    else:
                        dst[r, now] = value

    def halo_levels():
        tile = pl.ds(FIRST - 1, 1)
        for even in range(0, NB, 2):
            base, over = normed(even, tile), normed(even + 1, tile)
            for k in range(2):
                s1[even + k, tile] = jnp.where(t > 0, base + pltpu.roll(over, delay[0, even + k], 1), 0.0)
        for level, src, dst in ((1, s1, s2), (2, s2, s3)):
            for r in range(NB):
                lo, hi = pick(level, r)
                dst[r, tile] = src[lo, tile] + pltpu.roll(src[hi, tile], delay[level, r], 1)

    landed = head.at[pl.ds(0, NZ - 1), pl.ds(0, NQ + 1)]
    pltpu.make_async_copy(landed, landed, z_recv).wait()
    for r in range(1, NQ):
        there = {"band": z * NQ + turned[r]}
        for i, (src, dst) in enumerate((
            (head.at[:, pl.ds(turned[r], 1)], tiles.at[:, pl.ds(q, 1)]), (head.at[:, pl.ds(NQ, 1)], stat_q.at[:, pl.ds(q, 1)])
        )):
            pltpu.make_async_remote_copy(
                src_ref=src, dst_ref=dst, send_sem=q_send.at[i], recv_sem=q_recv.at[i], device_id=there, device_id_type=MESH
            ).start()
    tiles[:, pl.ds(q, 1)] = head[:, pl.ds(q, 1)]
    stat_q[:, pl.ds(q, 1)] = head[:, pl.ds(NQ, 1)]
    for i, dst in enumerate((tiles, stat_q)):
        part = dst.at[:, pl.ds(0, NQ - 1)]
        pltpu.make_async_copy(part, part, q_recv.at[i]).wait()

    halo = pltpu.make_async_remote_copy(
        src_ref=tiles, dst_ref=before_first, send_sem=halo_send, recv_sem=halo_recv, device_id={"tm": t_peers[0]},
        device_id_type=MESH,
    )
    halo.start()
    stat_t[pl.ds(t, 1)] = as_row(*as_columns(stat_q[...].reshape(NB, 128), me))[None]
    t_copies = []
    for i, k in enumerate(t_peers):
        t_copies.append(pltpu.make_async_remote_copy(
            src_ref=stat_t.at[t], dst_ref=stat_t.at[t], send_sem=t_send.at[i], recv_sem=t_recv.at[i],
            device_id={"tm": k}, device_id_type=MESH,
        ))
        t_copies[-1].start()
    for copy in t_copies:
        copy.wait_recv()
    stat = stat_t[0]
    for i in range(1, NT):
        stat = stat + stat_t[i]
    mean, inv = as_columns(stat, row)
    means[...] = jnp.broadcast_to(mean, (NB, 128))
    invs[...] = jnp.broadcast_to(inv, (NB, 128))
    for copy in tables:
        copy.wait()
    halo.wait_recv()
    buf[:, FIRST - 1, :] = before_first[...].reshape(NB, 128)
    buf[:, ROWS - 1, :] = tiles[...].reshape(NB, 128)
    halo_levels()
    def settle():
        halo.wait_send()
        for copy in t_copies:
            copy.wait_send()
        pltpu.make_async_copy(landed, landed, z_send).wait()
        for i, dst in enumerate((tiles, stat_q)):
            part = dst.at[:, pl.ds(0, NQ - 1)]
            pltpu.make_async_copy(part, part, q_send.at[i]).wait()

    def merge(order):
        for g in order:
            if g == order[-1]:
                settle()
            arrive(g)
            levels(g)

    far_last = (z < NZ // 2) | (z == 5)
    pl.when(far_last)(lambda: merge((0, 1, 2, 3)))
    pl.when(jnp.logical_not(far_last))(lambda: merge((3, 2, 0, 1)))

    rows = buf.at[pl.ds(0, NB - 1), pl.ds(FIRST, BODY)]
    pltpu.make_async_copy(rows, rows, send_sem).wait()


def shards(spectra, newest, ingest_owner, low_trial, high_trial, delay_table):
    operands = [spectra.reshape(NB, TILES, 128), newest.reshape(NB, 8, 128)]
    operands += [ingest_owner, low_trial, high_trial, delay_table]
    operands = [a if a.size == 1 else pltpu.with_memory_space_constraint(a, pltpu.HBM) for a in operands]
    state = pltpu.VMEM((NB, ROWS, 128), jnp.float32)
    table = pltpu.SMEM((LEVELS, NB), jnp.int32)
    square = pltpu.VMEM((NZ, NQ, 128), jnp.float32)
    out = pl.pallas_call(
        kernel,
        out_shape=jax.ShapeDtypeStruct((NB, TILES, 128), jnp.float32),
        in_specs=[pl.BlockSpec(memory_space=pltpu.SMEM if a.size == 1 else pl.ANY) for a in operands],
        out_specs=pl.BlockSpec(memory_space=pltpu.VMEM),
        scratch_shapes=[
            state,
            pltpu.VMEM((NB, 8, 128), jnp.float32),
            pltpu.VMEM((NZ, 2 * NQ, 128), jnp.float32),
            pltpu.VMEM((NZ, 2 * NQ, 128), jnp.float32),
            square, square, square,
            pltpu.VMEM((NB, 8, 128), jnp.float32),
            pltpu.VMEM((NT, 1, 128), jnp.float32),
            pltpu.VMEM((NB, 128), jnp.float32),
            pltpu.VMEM((NB, 128), jnp.float32),
            state, state, state,
            table, table, table,
            pltpu.SemaphoreType.DMA((5,)),
            pltpu.SemaphoreType.DMA,
            pltpu.SemaphoreType.DMA((GROUPS,)),
            pltpu.SemaphoreType.DMA,
            pltpu.SemaphoreType.DMA,
            pltpu.SemaphoreType.DMA((2,)),
            pltpu.SemaphoreType.DMA((2,)),
            pltpu.SemaphoreType.DMA((NT - 1,)),
            pltpu.SemaphoreType.DMA((NT - 1,)),
            pltpu.SemaphoreType.DMA,
            pltpu.SemaphoreType.DMA,
        ],
        compiler_params=pltpu.CompilerParams(collective_id=1, has_side_effects=True, vmem_limit_bytes=24 << 20),
    )(*operands)
    return out.reshape(NB // 16, 16, TILES * 128)


def solution(mesh):
    return jax.shard_map(
        shards,
        mesh=mesh,
        in_specs=(
            P(None, "band", "tm"),
            P(None, "band", "tm", None),
            P("band"),
            P(None, "band"),
            P(None, "band"),
            P(None, "band"),
        ),
        out_specs=P("band", None, "tm"),
        check_vma=False,
    )
```
